32 devices in a mesh: groups: 2 (over x), tensor: 8 (over z, y), side: 2 (over core).
Axes of the slice: x: 2, y: 2, z: 4, core: 2. Of those that a mesh axis runs over, the one named last changes fastest.
Arguments:
- hidden: bfloat16 [4, 64, 5120], P(None, ('groups', 'tensor', 'side')), parts along dimension 1, may hold values from -6 to 6
- norm_gain: float32 [5120], replicated, may hold values from 0.5 to 1.5
- query_gain: float32 [128], replicated, may hold values from 0.5 to 120
- key_gain: float32 [128], replicated, may hold values from 0.5 to 3
- w_query: bfloat16 [5120, 8192], P(('tensor', 'side')), may hold values from -0.078125 to 0.078125
- w_key: bfloat16 [5120, 1024], P(('tensor', 'side')), may hold values from -0.078125 to 0.078125
- w_value: bfloat16 [5120, 1024], P(('tensor', 'side')), may hold values from -0.078125 to 0.078125
- w_out: bfloat16 [8192, 5120], P(None, ('tensor', 'side')), may hold values from -0.0625 to 0.0625
- cache_k: bfloat16 [64, 8, 512, 128], P(('groups', 'tensor', 'side')), parts along dimension 0, may hold values from -6 to 6
- cache_v: bfloat16 [64, 8, 512, 128], P(('groups', 'tensor', 'side')), parts along dimension 0, may hold values from -6 to 6
- lengths: int32 [64], P(('groups', 'tensor', 'side')), parts along dimension 0, may hold values from 1 to 512, 8192 in all
Outputs:
- layer_out: bfloat16 [4, 64, 5120], P(None, ('groups', 'tensor', 'side')), parts along dimension 1
The draws below stay inside these ranges and needn't reach their ends.
There are 2 independent parts, one for each index of `groups`. The reference program is written for one: setup_inputs(seed, part) draws one part's arguments, and reference() takes and returns one part's arrays. A program takes and returns all parts, laid end to end along the dimension named above; an argument that names none is the same for every part. Nothing has to cross between parts.
Inputs may be any that keep to these rules, and one draw needn't show every extreme that they name: `lengths`: each row's count of cached positions in use; within each job the 32 rows' counts sum to 8192, and in each job the largest row uses all 512.
All inputs are finite; a program needn't handle non-finite values. No bound on the sum of `lengths` on one device may be relied on, other than what follows from the above.
Results may differ from the reference program's by a relative error of at most 0.013.
The reference program's roundings to bfloat16 on the way count: a program that leaves them out, or rounds other values in their place, can miss the bound.
Values may be sent and summed in bfloat16 or wider, within the bound.
A program may use at most 192 MiB of HBM per device.

```python
import math
import jax
import jax.numpy as jnp
import numpy as np
from jax import lax

D = 5120
HEADS = 64
KV_HEADS = 8
HEAD_DIM = 128
CTX = 512
STEPS = 4
ROWS = 32


def draw_query_gain(key, part):
    key = jax.random.fold_in(key, 11)
    low_end = 0.5
    high_end = 3.0
    spread = jax.random.uniform(key, (HEAD_DIM,), jnp.float32)
    return jnp.exp(math.log(low_end) + spread * (math.log(high_end) - math.log(low_end))).astype(jnp.float32)


def level_of(own_key, extent, shards, least, top_value):
    gain, own = 1.0, jax.random.fold_in(own_key, 6)
    for dim, blocks in shards:
        steps = jnp.exp(jax.random.uniform(jax.random.fold_in(own, dim), (blocks,), jnp.float32, least / len(shards), top_value / len(shards)))
        gain = gain * jnp.repeat(steps, extent[dim] // blocks).reshape([-1 if axis == dim else 1 for axis in range(len(extent))])
    return gain


def profile(number_of, total, bound, slope):
    weights = [(1 << 20) // math.isqrt(rank ** slope) + 1 for rank in range(2, number_of + 1)]
    rest, given = total - bound - (number_of - 1), [1] * (number_of - 1)
    while rest > 0:
        candidates = [i for i in range(number_of - 1) if given[i] < bound]
        pool, remaining = sum([weights[i] for i in candidates]), rest
        for i in candidates:
            extra = min(bound - given[i], max(1, remaining * weights[i] // pool), rest)
            given[i] = given[i] + extra
            rest = rest - extra
    return np.array([bound] + given)


def uneven(rng, count, total, most, lean):
    if count == 2:
        one = jax.random.randint(rng, (), max(1, total - most), min(most, total - 1) + 1)
        return jnp.stack([one, total - one])
    sizes = jnp.asarray(profile(count, total, most, lean), jnp.int32)
    pairs = (count - 1) // 2
    donor, receiver = sizes[1:1 + 2 * pairs:2], sizes[2:2 + 2 * pairs:2]
    margin = jnp.minimum(donor - 1, most - receiver)
    passed = jax.random.randint(jax.random.fold_in(rng, 1), (pairs,), 0, 1 << 20) % (margin + 1)
    sizes = sizes.at[1:1 + 2 * pairs:2].set(donor - passed).at[2:2 + 2 * pairs:2].set(receiver + passed)
    return sizes[jax.random.permutation(jax.random.fold_in(rng, 2), count)]


def scatter_about(own_key, shape, scale, bound, pieces=(), held_as=jnp.bfloat16):
    drawn = scale * jax.random.normal(own_key, shape, jnp.float32)
    if pieces:
        drawn = drawn * level_of(own_key, shape, pieces, -0.22, 0.18)
    return jnp.clip(drawn, -bound, bound).astype(held_as)


def setup_inputs(seed: int = 0, part: int = 0) -> dict:
    splits = jax.random.split(jax.random.key(seed), 12)
    part_keys = jax.random.split(jax.random.fold_in(splits[11], part), 12)
    hidden = scatter_about(part_keys[0], (STEPS, ROWS, D), 1.0, 6.0, ((1, 16),))
    norm_gain = jnp.clip(1.0 + 0.1 * jax.random.normal(splits[1], (D,), jnp.float32), 0.5, 1.5)
    query_gain = draw_query_gain(jax.random.fold_in(splits[11], 71), part)
    key_gain = jnp.clip(jnp.exp(jax.random.uniform(splits[3], (HEAD_DIM,), jnp.float32, math.log(0.5), math.log(3.0))), 0.5, 3.0)
    w_query = scatter_about(splits[4], (D, HEADS * HEAD_DIM), D ** -0.5, 0.078125, ((0, 16),))
    w_key = scatter_about(splits[5], (D, KV_HEADS * HEAD_DIM), D ** -0.5, 0.078125, ((0, 16),))
    w_value = scatter_about(splits[6], (D, KV_HEADS * HEAD_DIM), D ** -0.5, 0.078125, ((0, 16),))
    w_out = scatter_about(splits[7], (HEADS * HEAD_DIM, D), (HEADS * HEAD_DIM) ** -0.5, 0.0625, ((1, 16),))
    cache_k = scatter_about(part_keys[8], (ROWS, KV_HEADS, CTX, HEAD_DIM), 1.0, 6.0, ((0, 16),))
    cache_v = scatter_about(part_keys[9], (ROWS, KV_HEADS, CTX, HEAD_DIM), 1.0, 6.0, ((0, 16),))
    lengths = uneven(part_keys[10], ROWS, ROWS * CTX // 2, CTX, 2).astype(jnp.int32)
    return dict(hidden=hidden, norm_gain=norm_gain, query_gain=query_gain, key_gain=key_gain, w_query=w_query, w_key=w_key, w_value=w_value, w_out=w_out, cache_k=cache_k, cache_v=cache_v, lengths=lengths)


rope_base = 1000000.0
norm_eps = 1e-06
masked_score = -1e+30

def rms_scale(values, gain_vector):
    mean_square = lax.optimization_barrier(jnp.mean(values * values, axis=-1, keepdims=True))
    return values * lax.rsqrt(mean_square + norm_eps) * gain_vector

def rotate(values, positions):
    half_dim = values.shape[-1] // 2
    frequency = rope_base ** (-2.0 * jnp.arange(half_dim, dtype=jnp.float32) / values.shape[-1])
    angles = positions[:, None] * frequency[None, :]
    cosine = jnp.cos(angles)[:, None, :]
    sine_part = jnp.sin(angles)[:, None, :]
    lower_half = values[..., :half_dim]
    upper_half = values[..., half_dim:]
    return jnp.concatenate([lower_half * cosine - upper_half * sine_part, upper_half * cosine + lower_half * sine_part], axis=-1)

def attend(queries, cache_k, cache_v, lengths, fresh_k, fresh_v):
    row_count, head_count, head_size = queries.shape
    kv_count = cache_k.shape[1]
    grouped = queries.reshape(row_count, kv_count, head_count // kv_count, head_size).astype(jnp.float32)
    score_scale = head_size ** (-0.5)
    cached_scores = jnp.einsum('rkgd,rkld->rkgl', grouped, cache_k.astype(jnp.float32)) * score_scale
    live_mask = jnp.arange(cache_k.shape[2], dtype=jnp.int32)[None, :] < lengths[:, None]
    cached_scores = jnp.where(live_mask[:, None, None, :], cached_scores, masked_score)
    fresh_scores = jnp.einsum('rkgd,rksd->rkgs', grouped, fresh_k.astype(jnp.float32)) * score_scale
    highest = jnp.maximum(lax.optimization_barrier(jnp.max(cached_scores, axis=-1)), lax.optimization_barrier(jnp.max(fresh_scores, axis=-1)))[..., None]
    cached_exp = jnp.exp(cached_scores - highest)
    fresh_exp = jnp.exp(fresh_scores - highest)
    denominator = lax.optimization_barrier(jnp.sum(cached_exp, axis=-1, keepdims=True)) + lax.optimization_barrier(jnp.sum(fresh_exp, axis=-1, keepdims=True))
    cached_weight = (cached_exp / denominator).astype(jnp.bfloat16)
    fresh_weight = (fresh_exp / denominator).astype(jnp.bfloat16)
    mixed_out = jnp.einsum('rkgl,rkld->rkgd', cached_weight.astype(jnp.float32), cache_v.astype(jnp.float32))
    mixed_out = mixed_out + jnp.einsum('rkgs,rksd->rkgd', fresh_weight.astype(jnp.float32), fresh_v.astype(jnp.float32))
    return mixed_out.reshape(row_count, head_count * head_size).astype(jnp.bfloat16)

def reference(hidden, norm_gain, query_gain, key_gain, w_query, w_key, w_value, w_out, cache_k, cache_v, lengths):
    joined_weight = jnp.concatenate([w_query, w_key, w_value], axis=1)
    query_width = HEADS * HEAD_DIM
    key_width = KV_HEADS * HEAD_DIM
    row_total = hidden.shape[1]
    positions = lengths.astype(jnp.float32)
    fresh_keys = []
    fresh_values = []
    outputs = []
    for step_index in range(STEPS):
        residual = hidden[step_index].astype(jnp.float32)
        normed = rms_scale(residual, norm_gain.astype(jnp.float32)).astype(jnp.bfloat16)
        projected = jnp.dot(normed, joined_weight, preferred_element_type=jnp.float32).astype(jnp.bfloat16)
        q_rows = projected[:, :query_width].astype(jnp.float32).reshape(row_total, HEADS, HEAD_DIM)
        k_rows = projected[:, query_width:query_width + key_width].astype(jnp.float32).reshape(row_total, KV_HEADS, HEAD_DIM)
        v_rows = projected[:, query_width + key_width:].reshape(row_total, KV_HEADS, HEAD_DIM)
        queries = rotate(rms_scale(q_rows, query_gain.astype(jnp.float32)), positions + step_index).astype(jnp.bfloat16)
        keys_new = rotate(rms_scale(k_rows, key_gain.astype(jnp.float32)), positions + step_index).astype(jnp.bfloat16)
        fresh_keys.append(keys_new)
        fresh_values.append(v_rows)
        attended = attend(queries, cache_k, cache_v, lengths, jnp.stack(fresh_keys, axis=2), jnp.stack(fresh_values, axis=2))
        update = jnp.dot(attended, w_out, preferred_element_type=jnp.float32)
        outputs.append((residual + update).astype(jnp.bfloat16))
    return jnp.stack(outputs, axis=0)
```

```python
import jax
import jax.numpy as jnp
from jax import lax
from jax.sharding import PartitionSpec as P

rope_base = 1000000.0
norm_eps = 1e-06
masked_score = -1e30
ring = ("tensor", "side")


def rms_scale(values, gain_vector):
    mean_square = jnp.mean(values * values, axis=-1, keepdims=True)
    return values * lax.rsqrt(mean_square + norm_eps) * gain_vector


def rotate(values, positions):
    half_dim = values.shape[-1] // 2
    frequency = rope_base ** (-2.0 * jnp.arange(half_dim, dtype=jnp.float32) / values.shape[-1])
    angles = positions[..., None] * frequency
    cosine = jnp.cos(angles)[..., None, :]
    sine_part = jnp.sin(angles)[..., None, :]
    lower_half = values[..., :half_dim]
    upper_half = values[..., half_dim:]
    return jnp.concatenate(
        [
            lower_half * cosine - upper_half * sine_part,
            upper_half * cosine + lower_half * sine_part,
        ],
        axis=-1,
    )


def attend(queries, cache_k, cache_v, lengths, fresh_k, fresh_v):
    step_total, row_count, head_count, head_size = queries.shape
    kv_count, context = cache_k.shape[1:3]
    group = head_count // kv_count
    grouped = queries.reshape(step_total, row_count, kv_count, group, head_size)
    grouped = grouped.transpose(1, 2, 0, 3, 4).reshape(
        row_count, kv_count, step_total * group, head_size
    )
    fresh_k = fresh_k.transpose(1, 2, 0, 3)
    fresh_v = fresh_v.transpose(1, 2, 0, 3)
    score_scale = head_size ** (-0.5)
    cached_scores = (
        jnp.einsum("rkqd,rkld->rkql", grouped, cache_k, preferred_element_type=jnp.float32)
        * score_scale
    )
    live_mask = jnp.arange(context, dtype=jnp.int32)[None, :] < lengths[:, None]
    cached_scores = jnp.where(live_mask[:, None, None, :], cached_scores, masked_score)
    fresh_scores = (
        jnp.einsum("rkqd,rksd->rkqs", grouped, fresh_k, preferred_element_type=jnp.float32)
        * score_scale
    )
    query_step = jnp.arange(step_total * group, dtype=jnp.int32) // group
    causal = jnp.arange(step_total, dtype=jnp.int32)[None, :] <= query_step[:, None]
    fresh_scores = jnp.where(causal, fresh_scores, masked_score)
    highest = jnp.maximum(jnp.max(cached_scores, axis=-1), jnp.max(fresh_scores, axis=-1))[
        ..., None
    ]
    cached_exp = jnp.exp(cached_scores - highest)
    fresh_exp = jnp.exp(fresh_scores - highest)
    denominator = jnp.sum(cached_exp, axis=-1, keepdims=True) + jnp.sum(
        fresh_exp, axis=-1, keepdims=True
    )
    cached_weight = (cached_exp / denominator).astype(jnp.bfloat16)
    fresh_weight = (fresh_exp / denominator).astype(jnp.bfloat16)
    mixed_out = jnp.einsum(
        "rkql,rkld->rkqd", cached_weight, cache_v, preferred_element_type=jnp.float32
    )
    mixed_out = mixed_out + jnp.einsum(
        "rkqs,rksd->rkqd", fresh_weight, fresh_v, preferred_element_type=jnp.float32
    )
    mixed_out = mixed_out.astype(jnp.bfloat16)
    mixed_out = mixed_out.reshape(row_count, kv_count, step_total, group, head_size)
    return mixed_out.transpose(2, 0, 1, 3, 4).reshape(
        step_total * row_count, head_count * head_size
    )


def body(
    hidden,
    norm_gain,
    query_gain,
    key_gain,
    w_query,
    w_key,
    w_value,
    w_out,
    cache_k,
    cache_v,
    lengths,
):
    step_total, row_count, model_width = hidden.shape
    own_rows = step_total * row_count
    head_size = query_gain.shape[0]
    query_width, key_width = w_query.shape[1], w_key.shape[1]
    residual = hidden.astype(jnp.float32)
    normed = rms_scale(residual, norm_gain).astype(jnp.bfloat16).reshape(own_rows, model_width)
    slab = lax.all_to_all(normed, ring, split_axis=1, concat_axis=0, tiled=True)
    partial_sums = jnp.concatenate(
        [
            jnp.dot(slab, weight, preferred_element_type=jnp.float32)
            for weight in (w_query, w_key, w_value)
        ],
        axis=1,
    )
    projected = lax.psum_scatter(partial_sums, ring, scatter_dimension=0, tiled=True).astype(
        jnp.bfloat16
    )
    q_heads = projected[:, :query_width].astype(jnp.float32)
    k_heads = projected[:, query_width : query_width + key_width].astype(jnp.float32)
    fresh_v = projected[:, query_width + key_width :]
    positions = lengths.astype(jnp.float32)[None, :] + jnp.arange(step_total, dtype=jnp.float32)[:, None]
    q_heads = q_heads.reshape(step_total, row_count, -1, head_size)
    k_heads = k_heads.reshape(step_total, row_count, -1, head_size)
    queries = rotate(rms_scale(q_heads, query_gain), positions).astype(jnp.bfloat16)
    fresh_k = rotate(rms_scale(k_heads, key_gain), positions).astype(jnp.bfloat16)
    fresh_v = fresh_v.reshape(step_total, row_count, -1, head_size)
    attended = attend(queries, cache_k, cache_v, lengths, fresh_k, fresh_v)
    everyone = lax.all_gather(attended, ring, axis=0, tiled=True)
    columns = jnp.dot(everyone, w_out, preferred_element_type=jnp.float32)
    update = lax.all_to_all(columns, ring, split_axis=0, concat_axis=1, tiled=True)
    update = update.reshape(step_total, row_count, model_width)
    return (residual + update).astype(jnp.bfloat16)


def solution(mesh):
    placed = (
        P(None, ("groups", "tensor", "side"), None),
        P(),
        P(),
        P(),
        P(("tensor", "side"), None),
        P(("tensor", "side"), None),
        P(("tensor", "side"), None),
        P(None, ("tensor", "side")),
        P(("groups", "tensor", "side"), None, None, None),
        P(("groups", "tensor", "side"), None, None, None),
        P(("groups", "tensor", "side")),
    )
    return jax.shard_map(
        body,
        mesh=mesh,
        in_specs=placed,
        out_specs=P(None, ("groups", "tensor", "side"), None),
        check_vma=False,
    )
```

```python
import functools

import jax
import jax.numpy as jnp
from jax import lax
from jax.experimental import pallas as pl
from jax.experimental.pallas import tpu as pltpu
from jax.sharding import PartitionSpec as P

rope_base = 1000000.0
norm_eps = 1e-06
masked_score = -1e30
ring = ("tensor", "side")


def rms_scale(values, gain_vector):
    mean_square = jnp.mean(values * values, axis=-1, keepdims=True)
    return values * lax.rsqrt(mean_square + norm_eps) * gain_vector


def rotate(values, positions):
    half_dim = values.shape[-1] // 2
    frequency = rope_base ** (-2.0 * jnp.arange(half_dim, dtype=jnp.float32) / values.shape[-1])
    angles = positions[..., None] * frequency
    cosine = jnp.cos(angles)[..., None, :]
    sine_part = jnp.sin(angles)[..., None, :]
    lower_half = values[..., :half_dim]
    upper_half = values[..., half_dim:]
    return jnp.concatenate(
        [
            lower_half * cosine - upper_half * sine_part,
            upper_half * cosine + lower_half * sine_part,
        ],
        axis=-1,
    )


def attend(queries, cache_k, cache_v, lengths, fresh_k, fresh_v):
    step_total, row_count, head_count, head_size = queries.shape
    kv_count, context = cache_k.shape[1:3]
    group = head_count // kv_count
    grouped = queries.reshape(step_total, row_count, kv_count, group, head_size)
    grouped = grouped.transpose(1, 2, 0, 3, 4).reshape(
        row_count, kv_count, step_total * group, head_size
    )
    fresh_k = fresh_k.transpose(1, 2, 0, 3)
    fresh_v = fresh_v.transpose(1, 2, 0, 3)
    score_scale = head_size ** (-0.5)
    cached_scores = (
        jnp.einsum("rkqd,rkld->rkql", grouped, cache_k, preferred_element_type=jnp.float32)
        * score_scale
    )
    live_mask = jnp.arange(context, dtype=jnp.int32)[None, :] < lengths[:, None]
    cached_scores = jnp.where(live_mask[:, None, None, :], cached_scores, masked_score)
    fresh_scores = (
        jnp.einsum("rkqd,rksd->rkqs", grouped, fresh_k, preferred_element_type=jnp.float32)
        * score_scale
    )
    query_step = jnp.arange(step_total * group, dtype=jnp.int32) // group
    causal = jnp.arange(step_total, dtype=jnp.int32)[None, :] <= query_step[:, None]
    fresh_scores = jnp.where(causal, fresh_scores, masked_score)
    highest = jnp.maximum(jnp.max(cached_scores, axis=-1), jnp.max(fresh_scores, axis=-1))[
        ..., None
    ]
    cached_exp = jnp.exp(cached_scores - highest)
    fresh_exp = jnp.exp(fresh_scores - highest)
    denominator = jnp.sum(cached_exp, axis=-1, keepdims=True) + jnp.sum(
        fresh_exp, axis=-1, keepdims=True
    )
    cached_weight = (cached_exp / denominator).astype(jnp.bfloat16)
    fresh_weight = (fresh_exp / denominator).astype(jnp.bfloat16)
    mixed_out = jnp.einsum(
        "rkql,rkld->rkqd", cached_weight, cache_v, preferred_element_type=jnp.float32
    )
    mixed_out = mixed_out + jnp.einsum(
        "rkqs,rksd->rkqd", fresh_weight, fresh_v, preferred_element_type=jnp.float32
    )
    mixed_out = mixed_out.astype(jnp.bfloat16)
    mixed_out = mixed_out.reshape(row_count, kv_count, step_total, group, head_size)
    return mixed_out.transpose(2, 0, 1, 3, 4).reshape(
        step_total * row_count, head_count * head_size
    )


LONG, SHORT, SIDE = 4, 2, 2
OWNERS = LONG * SHORT * SIDE
VMEM_BYTES = 56 * 1024 * 1024


def place():
    tensor_index = lax.axis_index("tensor")
    return tensor_index // SHORT, lax.rem(tensor_index, SHORT), lax.axis_index("side")


def others():
    return [
        (a, b, c)
        for a in range(LONG)
        for b in range(SHORT)
        for c in range(SIDE)
        if (a, b, c) != (0, 0, 0)
    ]


def slot(step):
    a, b, c = step
    return (a * SHORT + b) * SIDE + c


def shifted(me, step):
    return tuple(
        lax.rem(i + d, n) for i, d, n in zip(me, step, (LONG, SHORT, SIDE), strict=True)
    )


def device(where):
    return {"tensor": where[0] * SHORT + where[1], "side": where[2]}


def number(where):
    return (where[0] * SHORT + where[1]) * SIDE + where[2]


def by_side(where):
    return (where[2] * SHORT + where[1]) * LONG + where[0]


def remote(src, dst, send_sem, recv_sem, where):
    return pltpu.make_async_remote_copy(
        src_ref=src,
        dst_ref=dst,
        send_sem=send_sem,
        recv_sem=recv_sem,
        device_id=device(where),
        device_id_type=pl.DeviceIdType.MESH,
    )


def greet(me):
    barrier = pltpu.get_barrier_semaphore()
    for step in others():
        pl.semaphore_signal(
            barrier,
            inc=1,
            device_id=device(shifted(me, step)),
            device_id_type=pl.DeviceIdType.MESH,
        )
    pl.semaphore_wait(barrier, OWNERS - 1)


def project_kernel(
    width,
    x_ref,
    wq_ref,
    wk_ref,
    wv_ref,
    out_ref,
    wq,
    wk,
    wv,
    slab,
    first,
    from_side,
    second,
    from_short,
    third,
    from_long,
    load_sem,
    slab_send,
    slab_recv,
    send_sem,
    recv_sem,
):
    me = place()
    long_index, short_index, side_index = me
    loads = [
        pltpu.make_async_copy(src, dst, load_sem.at[i])
        for i, (src, dst) in enumerate(((wq_ref, wq), (wk_ref, wk), (wv_ref, wv)))
    ]
    for load in loads:
        load.start()
    greet(me)
    scattered = []
    for step in others():
        target = shifted(me, step)
        copy = remote(
            x_ref.at[number(target)],
            slab.at[by_side(me)],
            slab_send.at[slot(step)],
            slab_recv.at[slot(step)],
            target,
        )
        copy.start()
        scattered.append(copy)
    slab[by_side(me)] = x_ref[number(me)]
    for load in loads:
        load.wait()
    for copy in scattered:
        copy.wait_recv()
    own_rows, depth = slab.shape[1:]
    left = slab[...].reshape(OWNERS * own_rows, depth).astype(jnp.bfloat16)

    pieces = []
    for weight in (wq, wk, wv):
        pieces += [(weight, start) for start in range(0, weight.shape[1], width)]
    total = len(pieces)
    sent = []

    def multiply(c):
        weight, start = pieces[c]
        product = jnp.dot(
            left, weight[:, start : start + width], preferred_element_type=jnp.float32
        )
        first[c] = product.reshape(SIDE, SHORT, LONG, own_rows, width)
        copy = remote(
            first.at[c, 1 - side_index],
            from_side.at[c],
            send_sem.at[c, 0],
            recv_sem.at[c, 0],
            shifted(me, (0, 0, 1)),
        )
        copy.start()
        sent.append(copy)
        return copy

    def add_side(c, arrived):
        arrived.wait_recv()
        second[c] = first[c, side_index] + from_side[c]
        copy = remote(
            second.at[c, 1 - short_index],
            from_short.at[c],
            send_sem.at[c, 1],
            recv_sem.at[c, 1],
            shifted(me, (0, 1, 0)),
        )
        copy.start()
        sent.append(copy)
        return copy

    def add_short(c, arrived):
        arrived.wait_recv()
        third[c] = second[c, short_index] + from_short[c]
        copies = []
        for hop in range(1, LONG):
            target = shifted(me, (hop, 0, 0))
            copy = remote(
                third.at[c, target[0]],
                from_long.at[c, hop - 1],
                send_sem.at[c, 1 + hop],
                recv_sem.at[c, 1 + hop],
                target,
            )
            copy.start()
            copies.append(copy)
        sent.extend(copies)
        return copies

    def add_long(c, arrived):
        value = third[c, long_index]
        for hop, copy in enumerate(arrived):
            copy.wait_recv()
            value = value + from_long[c, hop]
        out_ref[:, c * width : (c + 1) * width] = value

    side_copies = [None] * total
    short_copies = [None] * total
    long_copies = [None] * total
    for tick in range(total + 4):
        if tick < total:
            side_copies[tick] = multiply(tick)
        if 0 <= tick - 1 < total:
            short_copies[tick - 1] = add_side(tick - 1, side_copies[tick - 1])
        if 0 <= tick - 3 < total:
            long_copies[tick - 3] = add_short(tick - 3, short_copies[tick - 3])
        if 0 <= tick - 4 < total:
            add_long(tick - 4, long_copies[tick - 4])
    for copy in scattered + sent:
        copy.wait_send()


def project(blocks, w_query, w_key, w_value):
    own_rows, depth = blocks.shape[1:]
    width = w_key.shape[1]
    columns = w_query.shape[1] + w_key.shape[1] + w_value.shape[1]
    total = columns // width
    f32 = jnp.float32
    hbm = pl.BlockSpec(memory_space=pl.ANY)
    vmem = pl.BlockSpec(memory_space=pltpu.VMEM)
    return pl.pallas_call(
        functools.partial(project_kernel, width),
        out_shape=jax.ShapeDtypeStruct((own_rows, columns), f32),
        in_specs=[vmem, hbm, hbm, hbm],
        out_specs=vmem,
        scratch_shapes=[
            pltpu.VMEM(w_query.shape, w_query.dtype),
            pltpu.VMEM(w_key.shape, w_key.dtype),
            pltpu.VMEM(w_value.shape, w_value.dtype),
            pltpu.VMEM(blocks.shape, f32),
            pltpu.VMEM((total, SIDE, SHORT, LONG, own_rows, width), f32),
            pltpu.VMEM((total, SHORT, LONG, own_rows, width), f32),
            pltpu.VMEM((total, SHORT, LONG, own_rows, width), f32),
            pltpu.VMEM((total, LONG, own_rows, width), f32),
            pltpu.VMEM((total, LONG, own_rows, width), f32),
            pltpu.VMEM((total, LONG - 1, own_rows, width), f32),
            pltpu.SemaphoreType.DMA((3,)),
            pltpu.SemaphoreType.DMA((OWNERS,)),
            pltpu.SemaphoreType.DMA((OWNERS,)),
            pltpu.SemaphoreType.DMA((total, 1 + LONG)),
            pltpu.SemaphoreType.DMA((total, 1 + LONG)),
        ],
        compiler_params=pltpu.CompilerParams(
            collective_id=0, has_side_effects=True, vmem_limit_bytes=VMEM_BYTES
        ),
    )(blocks, w_query, w_key, w_value)


def output_kernel(
    tile,
    x_ref,
    w_ref,
    out_ref,
    weight,
    gathered,
    low,
    high,
    result,
    load_sem,
    own_sem,
    send_sem,
    recv_sem,
    back_send,
    back_recv,
):
    me = place()
    load = pltpu.make_async_copy(w_ref, weight, load_sem)
    load.start()
    own = pltpu.make_async_copy(x_ref, gathered.at[number(me)], own_sem)
    own.start()
    greet(me)
    own.wait()
    copies = {}

    def pass_on(origin_step, step):
        behind = tuple((n - d) % n for d, n in zip(origin_step, (LONG, SHORT, SIDE)))
        block = gathered.at[number(shifted(me, behind))]
        arrival = tuple(o + d for o, d in zip(origin_step, step))
        copy = remote(
            block,
            block,
            send_sem.at[slot(arrival)],
            recv_sem.at[slot(arrival)],
            shifted(me, step),
        )
        copy.start()
        copies[arrival] = copy

    for hop in (2, 1, 3):
        pass_on((0, 0, 0), (hop, 0, 0))
    pass_on((0, 0, 0), (0, 1, 0))
    pass_on((0, 0, 0), (0, 0, 1))
    for hop in (1, 3, 2):
        copies[(hop, 0, 0)].wait_recv()
        pass_on((hop, 0, 0), (0, 1, 0))
        pass_on((hop, 0, 0), (0, 0, 1))
    for hop in (0, 1, 3, 2):
        copies[(hop, 1, 0)].wait_recv()
        pass_on((hop, 1, 0), (0, 0, 1))
    for hop in range(LONG):
        for short in range(SHORT):
            copies[(hop, short, 1)].wait_recv()
    load.wait()

    owners, block_rows, half = gathered.shape
    low[...] = jnp.zeros_like(low)
    high[...] = jnp.zeros_like(high)

    @pl.loop(0, half // tile)
    def _(index):
        start = pl.multiple_of(index * tile, tile)
        left = gathered[:, :, pl.ds(start, tile)].reshape(owners * block_rows, tile)
        upper = pl.multiple_of(half + index * tile, tile)
        low[...] += jnp.dot(
            left, weight[pl.ds(start, tile), :], preferred_element_type=jnp.float32
        )
        high[...] += jnp.dot(
            left, weight[pl.ds(upper, tile), :], preferred_element_type=jnp.float32
        )

    own_rows = block_rows // 2
    wide = (owners, block_rows, low.shape[1])
    result[...] = (
        low[...].reshape(wide)[:, :own_rows] + high[...].reshape(wide)[:, own_rows:]
    )
    returned = []
    for step in others():
        target = shifted(me, step)
        copy = remote(
            result.at[number(target)],
            out_ref.at[number(me)],
            back_send.at[slot(step)],
            back_recv.at[slot(step)],
            target,
        )
        copy.start()
        returned.append(copy)
    out_ref[number(me)] = result[number(me)]
    for copy in returned:
        copy.wait_recv()
    for copy in list(copies.values()) + returned:
        copy.wait_send()


def output(block, w_out):
    block_rows, half = block.shape
    columns = w_out.shape[1]
    tile = half // 8
    f32 = jnp.float32
    vmem = pl.BlockSpec(memory_space=pltpu.VMEM)
    return pl.pallas_call(
        functools.partial(output_kernel, tile),
        out_shape=jax.ShapeDtypeStruct((OWNERS, block_rows // 2, columns), f32),
        in_specs=[vmem, pl.BlockSpec(memory_space=pl.ANY)],
        out_specs=vmem,
        scratch_shapes=[
            pltpu.VMEM(w_out.shape, w_out.dtype),
            pltpu.VMEM((OWNERS, block_rows, half), block.dtype),
            pltpu.VMEM((OWNERS * block_rows, columns), f32),
            pltpu.VMEM((OWNERS * block_rows, columns), f32),
            pltpu.VMEM((OWNERS, block_rows // 2, columns), f32),
            pltpu.SemaphoreType.DMA,
            pltpu.SemaphoreType.DMA,
            pltpu.SemaphoreType.DMA((OWNERS,)),
            pltpu.SemaphoreType.DMA((OWNERS,)),
            pltpu.SemaphoreType.DMA((OWNERS,)),
            pltpu.SemaphoreType.DMA((OWNERS,)),
        ],
        compiler_params=pltpu.CompilerParams(
            collective_id=1, has_side_effects=True, vmem_limit_bytes=VMEM_BYTES
        ),
    )(block, w_out)


def body(
    direct,
    hidden,
    norm_gain,
    query_gain,
    key_gain,
    w_query,
    w_key,
    w_value,
    w_out,
    cache_k,
    cache_v,
    lengths,
):
    step_total, row_count, model_width = hidden.shape
    own_rows = step_total * row_count
    head_size = query_gain.shape[0]
    query_width, key_width = w_query.shape[1], w_key.shape[1]
    residual = hidden.astype(jnp.float32)
    normed = rms_scale(residual, norm_gain).astype(jnp.bfloat16).reshape(own_rows, model_width)
    if direct:
        blocks = normed.astype(jnp.float32).reshape(own_rows, OWNERS, -1).transpose(1, 0, 2)
        projected = project(blocks, w_query, w_key, w_value)
    else:
        slab = lax.all_to_all(normed, ring, split_axis=1, concat_axis=0, tiled=True)
        partial_sums = jnp.concatenate(
            [
                jnp.dot(slab, weight, preferred_element_type=jnp.float32)
                for weight in (w_query, w_key, w_value)
            ],
            axis=1,
        )
        projected = lax.psum_scatter(partial_sums, ring, scatter_dimension=0, tiled=True)
    projected = projected.astype(jnp.bfloat16)
    q_heads = projected[:, :query_width].astype(jnp.float32)
    k_heads = projected[:, query_width : query_width + key_width].astype(jnp.float32)
    fresh_v = projected[:, query_width + key_width :]
    positions = lengths.astype(jnp.float32)[None, :] + jnp.arange(step_total, dtype=jnp.float32)[:, None]
    q_heads = q_heads.reshape(step_total, row_count, -1, head_size)
    k_heads = k_heads.reshape(step_total, row_count, -1, head_size)
    queries = rotate(rms_scale(q_heads, query_gain), positions).astype(jnp.bfloat16)
    fresh_k = rotate(rms_scale(k_heads, key_gain), positions).astype(jnp.bfloat16)
    fresh_v = fresh_v.reshape(step_total, row_count, -1, head_size)
    attended = attend(queries, cache_k, cache_v, lengths, fresh_k, fresh_v)
    if direct:
        halves = attended.reshape(own_rows, 2, -1).transpose(1, 0, 2).reshape(2 * own_rows, -1)
        update = output(halves, w_out).transpose(1, 0, 2)
    else:
        everyone = lax.all_gather(attended, ring, axis=0, tiled=True)
        columns = jnp.dot(everyone, w_out, preferred_element_type=jnp.float32)
        update = lax.all_to_all(columns, ring, split_axis=0, concat_axis=1, tiled=True)
    update = update.reshape(step_total, row_count, model_width)
    return (residual + update).astype(jnp.bfloat16)


def solution(mesh):
    placed = (
        P(None, ("groups", "tensor", "side"), None),
        P(),
        P(),
        P(),
        P(("tensor", "side"), None),
        P(("tensor", "side"), None),
        P(("tensor", "side"), None),
        P(None, ("tensor", "side")),
        P(("groups", "tensor", "side"), None, None, None),
        P(("groups", "tensor", "side"), None, None, None),
        P(("groups", "tensor", "side")),
    )
    direct = mesh.shape["tensor"] == LONG * SHORT and mesh.shape["side"] == SIDE
    return jax.shard_map(
        functools.partial(body, direct),
        mesh=mesh,
        in_specs=placed,
        out_specs=P(None, ("groups", "tensor", "side"), None),
        check_vma=False,
    )
```

```python
import functools

import jax
import jax.numpy as jnp
from jax import lax
from jax.experimental import pallas as pl
from jax.experimental.pallas import tpu as pltpu
from jax.sharding import PartitionSpec as P

rope_base = 1000000.0
norm_eps = 1e-06
masked_score = -1e30
ring = ("tensor", "side")


def rms_scale(values, gain_vector):
    mean_square = jnp.mean(values * values, axis=-1, keepdims=True)
    return values * lax.rsqrt(mean_square + norm_eps) * gain_vector


def rotate(values, positions):
    half_dim = values.shape[-1] // 2
    frequency = rope_base ** (-2.0 * jnp.arange(half_dim, dtype=jnp.float32) / values.shape[-1])
    angles = positions[..., None] * frequency
    cosine = jnp.cos(angles)[..., None, :]
    sine_part = jnp.sin(angles)[..., None, :]
    lower_half = values[..., :half_dim]
    upper_half = values[..., half_dim:]
    return jnp.concatenate(
        [
            lower_half * cosine - upper_half * sine_part,
            upper_half * cosine + lower_half * sine_part,
        ],
        axis=-1,
    )


def attend(queries, cache_k, cache_v, lengths, fresh_k, fresh_v):
    step_total, row_count, head_count, head_size = queries.shape
    kv_count, context = cache_k.shape[1:3]
    group = head_count // kv_count
    grouped = queries.reshape(step_total, row_count, kv_count, group, head_size)
    grouped = grouped.transpose(1, 2, 0, 3, 4).reshape(
        row_count, kv_count, step_total * group, head_size
    )
    fresh_k = fresh_k.transpose(1, 2, 0, 3)
    fresh_v = fresh_v.transpose(1, 2, 0, 3)
    score_scale = head_size ** (-0.5)
    cached_scores = (
        jnp.einsum("rkqd,rkld->rkql", grouped, cache_k, preferred_element_type=jnp.float32)
        * score_scale
    )
    live_mask = jnp.arange(context, dtype=jnp.int32)[None, :] < lengths[:, None]
    cached_scores = jnp.where(live_mask[:, None, None, :], cached_scores, masked_score)
    fresh_scores = (
        jnp.einsum("rkqd,rksd->rkqs", grouped, fresh_k, preferred_element_type=jnp.float32)
        * score_scale
    )
    query_step = jnp.arange(step_total * group, dtype=jnp.int32) // group
    causal = jnp.arange(step_total, dtype=jnp.int32)[None, :] <= query_step[:, None]
    fresh_scores = jnp.where(causal, fresh_scores, masked_score)
    highest = jnp.maximum(jnp.max(cached_scores, axis=-1), jnp.max(fresh_scores, axis=-1))[
        ..., None
    ]
    cached_exp = jnp.exp(cached_scores - highest)
    fresh_exp = jnp.exp(fresh_scores - highest)
    denominator = jnp.sum(cached_exp, axis=-1, keepdims=True) + jnp.sum(
        fresh_exp, axis=-1, keepdims=True
    )
    cached_weight = (cached_exp / denominator).astype(jnp.bfloat16)
    fresh_weight = (fresh_exp / denominator).astype(jnp.bfloat16)
    mixed_out = jnp.einsum(
        "rkql,rkld->rkqd", cached_weight, cache_v, preferred_element_type=jnp.float32
    )
    mixed_out = mixed_out + jnp.einsum(
        "rkqs,rksd->rkqd", fresh_weight, fresh_v, preferred_element_type=jnp.float32
    )
    mixed_out = mixed_out.astype(jnp.bfloat16)
    mixed_out = mixed_out.reshape(row_count, kv_count, step_total, group, head_size)
    return mixed_out.transpose(2, 0, 1, 3, 4).reshape(
        step_total * row_count, head_count * head_size
    )


LONG, SHORT, SIDE = 4, 2, 2
OWNERS = LONG * SHORT * SIDE
PIECES = 4
VMEM_BYTES = 56 * 1024 * 1024


def place():
    tensor_index = lax.axis_index("tensor")
    return tensor_index // SHORT, lax.rem(tensor_index, SHORT), lax.axis_index("side")


def others():
    return [
        (a, b, c)
        for a in range(LONG)
        for b in range(SHORT)
        for c in range(SIDE)
        if (a, b, c) != (0, 0, 0)
    ]


def slot(step):
    a, b, c = step
    return (a * SHORT + b) * SIDE + c


def shifted(me, step):
    return tuple(
        lax.rem(i + d, n) for i, d, n in zip(me, step, (LONG, SHORT, SIDE), strict=True)
    )


def device(where):
    return {"tensor": where[0] * SHORT + where[1], "side": where[2]}


def number(where):
    return (where[0] * SHORT + where[1]) * SIDE + where[2]


def by_side(where):
    return (where[2] * SHORT + where[1]) * LONG + where[0]


def remote(src, dst, send_sem, recv_sem, where):
    return pltpu.make_async_remote_copy(
        src_ref=src,
        dst_ref=dst,
        send_sem=send_sem,
        recv_sem=recv_sem,
        device_id=device(where),
        device_id_type=pl.DeviceIdType.MESH,
    )


def greet(me):
    barrier = pltpu.get_barrier_semaphore()
    for step in others():
        pl.semaphore_signal(
            barrier,
            inc=1,
            device_id=device(shifted(me, step)),
            device_id_type=pl.DeviceIdType.MESH,
        )
    pl.semaphore_wait(barrier, OWNERS - 1)


def project_kernel(
    width,
    x_ref,
    wq_ref,
    wk_ref,
    wv_ref,
    out_ref,
    wq,
    wk,
    wv,
    slab,
    first,
    from_side,
    second,
    from_short,
    third,
    from_long,
    load_sem,
    slab_send,
    slab_recv,
    send_sem,
    recv_sem,
):
    me = place()
    long_index, short_index, side_index = me
    loads = [
        pltpu.make_async_copy(src, dst, load_sem.at[i])
        for i, (src, dst) in enumerate(((wq_ref, wq), (wk_ref, wk), (wv_ref, wv)))
    ]
    for load in loads:
        load.start()
    greet(me)
    scattered = []
    for step in others():
        target = shifted(me, step)
        copy = remote(
            x_ref.at[number(target)],
            slab.at[by_side(me)],
            slab_send.at[slot(step)],
            slab_recv.at[slot(step)],
            target,
        )
        copy.start()
        scattered.append(copy)
    slab[by_side(me)] = x_ref[number(me)]
    for load in loads:
        load.wait()
    for copy in scattered:
        copy.wait_recv()
    own_rows, depth = slab.shape[1:]
    left = slab[...].reshape(OWNERS * own_rows, depth).astype(jnp.bfloat16)

    pieces = []
    for weight in (wq, wk, wv):
        pieces += [(weight, start) for start in range(0, weight.shape[1], width)]
    total = len(pieces)
    sent = []

    def multiply(c):
        weight, start = pieces[c]
        product = jnp.dot(
            left, weight[:, start : start + width], preferred_element_type=jnp.float32
        )
        first[c] = product.reshape(SIDE, SHORT, LONG, own_rows, width)
        copy = remote(
            first.at[c, 1 - side_index],
            from_side.at[c],
            send_sem.at[c, 0],
            recv_sem.at[c, 0],
            shifted(me, (0, 0, 1)),
        )
        copy.start()
        sent.append(copy)
        return copy

    def add_side(c, arrived):
        arrived.wait_recv()
        second[c] = first[c, side_index] + from_side[c]
        copy = remote(
            second.at[c, 1 - short_index],
            from_short.at[c],
            send_sem.at[c, 1],
            recv_sem.at[c, 1],
            shifted(me, (0, 1, 0)),
        )
        copy.start()
        sent.append(copy)
        return copy

    def add_short(c, arrived):
        arrived.wait_recv()
        third[c] = second[c, short_index] + from_short[c]
        copies = []
        for hop in range(1, LONG):
            target = shifted(me, (hop, 0, 0))
            copy = remote(
                third.at[c, target[0]],
                from_long.at[c, hop - 1],
                send_sem.at[c, 1 + hop],
                recv_sem.at[c, 1 + hop],
                target,
            )
            copy.start()
            copies.append(copy)
        sent.extend(copies)
        return copies

    def add_long(c, arrived):
        value = third[c, long_index]
        for hop, copy in enumerate(arrived):
            copy.wait_recv()
            value = value + from_long[c, hop]
        out_ref[:, c * width : (c + 1) * width] = value

    side_copies = [None] * total
    short_copies = [None] * total
    long_copies = [None] * total
    for tick in range(total + 6):
        if tick < total:
            side_copies[tick] = multiply(tick)
        if 0 <= tick - 1 < total:
            short_copies[tick - 1] = add_side(tick - 1, side_copies[tick - 1])
        if 0 <= tick - 3 < total:
            long_copies[tick - 3] = add_short(tick - 3, short_copies[tick - 3])
        if 0 <= tick - 6 < total:
            add_long(tick - 6, long_copies[tick - 6])
    for copy in scattered + sent:
        copy.wait_send()


def project(blocks, w_query, w_key, w_value):
    own_rows, depth = blocks.shape[1:]
    width = w_key.shape[1]
    columns = w_query.shape[1] + w_key.shape[1] + w_value.shape[1]
    total = columns // width
    f32 = jnp.float32
    hbm = pl.BlockSpec(memory_space=pl.ANY)
    vmem = pl.BlockSpec(memory_space=pltpu.VMEM)
    return pl.pallas_call(
        functools.partial(project_kernel, width),
        out_shape=jax.ShapeDtypeStruct((own_rows, columns), f32),
        in_specs=[vmem, hbm, hbm, hbm],
        out_specs=vmem,
        scratch_shapes=[
            pltpu.VMEM(w_query.shape, w_query.dtype),
            pltpu.VMEM(w_key.shape, w_key.dtype),
            pltpu.VMEM(w_value.shape, w_value.dtype),
            pltpu.VMEM(blocks.shape, f32),
            pltpu.VMEM((total, SIDE, SHORT, LONG, own_rows, width), f32),
            pltpu.VMEM((total, SHORT, LONG, own_rows, width), f32),
            pltpu.VMEM((total, SHORT, LONG, own_rows, width), f32),
            pltpu.VMEM((total, LONG, own_rows, width), f32),
            pltpu.VMEM((total, LONG, own_rows, width), f32),
            pltpu.VMEM((total, LONG - 1, own_rows, width), f32),
            pltpu.SemaphoreType.DMA((3,)),
            pltpu.SemaphoreType.DMA((OWNERS,)),
            pltpu.SemaphoreType.DMA((OWNERS,)),
            pltpu.SemaphoreType.DMA((total, 1 + LONG)),
            pltpu.SemaphoreType.DMA((total, 1 + LONG)),
        ],
        compiler_params=pltpu.CompilerParams(
            collective_id=0, has_side_effects=True, vmem_limit_bytes=VMEM_BYTES
        ),
    )(blocks, w_query, w_key, w_value)


def output_kernel(
    x_ref,
    w_ref,
    out_ref,
    weight,
    gathered,
    low,
    high,
    result,
    load_sem,
    own_sem,
    send_sem,
    recv_sem,
    back_send,
    back_recv,
):
    me = place()
    pieces, owners, block_rows, width = gathered.shape
    load = pltpu.make_async_copy(w_ref, weight, load_sem)
    load.start()
    own = [
        pltpu.make_async_copy(x_ref.at[p], gathered.at[p, number(me)], own_sem.at[p])
        for p in range(pieces)
    ]
    for copy in own:
        copy.start()
    greet(me)
    for copy in own:
        copy.wait()
    copies = {}

    def pass_on(p, origin_step, step):
        behind = tuple((n - d) % n for d, n in zip(origin_step, (LONG, SHORT, SIDE)))
        block = gathered.at[p, number(shifted(me, behind))]
        arrival = tuple(o + d for o, d in zip(origin_step, step))
        copy = remote(
            block,
            block,
            send_sem.at[p, slot(arrival)],
            recv_sem.at[p, slot(arrival)],
            shifted(me, step),
        )
        copy.start()
        copies[p, arrival] = copy

    def start_own(p):
        for hop in (2, 1, 3):
            pass_on(p, (0, 0, 0), (hop, 0, 0))
        pass_on(p, (0, 0, 0), (0, 1, 0))
        pass_on(p, (0, 0, 0), (0, 0, 1))

    def pass_long(p):
        for hop in (1, 3, 2):
            copies[p, (hop, 0, 0)].wait_recv()
            pass_on(p, (hop, 0, 0), (0, 1, 0))
            pass_on(p, (hop, 0, 0), (0, 0, 1))

    def pass_short(p):
        for hop in (0, 1, 3, 2):
            copies[p, (hop, 1, 0)].wait_recv()
            pass_on(p, (hop, 1, 0), (0, 0, 1))

    def multiply(p):
        for hop in range(LONG):
            for short in range(SHORT):
                copies[p, (hop, short, 1)].wait_recv()
        left = gathered[p].reshape(owners * block_rows, width)
        for total, start in ((low, p * width), (high, (pieces + p) * width)):
            product = lax.dot_general(
                left,
                weight[:, start : start + width],
                (((1,), (1,)), ((), ())),
                preferred_element_type=jnp.float32,
            )
            total[...] = product if p == 0 else total[...] + product

    for p in range(pieces):
        start_own(p)
    for tick in range(pieces + 2):
        if tick < pieces:
            pass_long(tick)
        if 0 <= tick - 1 < pieces:
            pass_short(tick - 1)
        if tick == 2:
            load.wait()
        if 0 <= tick - 2 < pieces:
            multiply(tick - 2)

    own_rows = block_rows // 2
    wide = (owners, block_rows, low.shape[1])
    result[...] = (
        low[...].reshape(wide)[:, :own_rows] + high[...].reshape(wide)[:, own_rows:]
    )
    returned = []
    for step in others():
        target = shifted(me, step)
        copy = remote(
            result.at[number(target)],
            out_ref.at[number(me)],
            back_send.at[slot(step)],
            back_recv.at[slot(step)],
            target,
        )
        copy.start()
        returned.append(copy)
    out_ref[number(me)] = result[number(me)]
    for copy in returned:
        copy.wait_recv()
    for copy in list(copies.values()) + returned:
        copy.wait_send()


def output(block, w_out):
    pieces, block_rows, width = block.shape
    columns = w_out.shape[1]
    f32 = jnp.float32
    vmem = pl.BlockSpec(memory_space=pltpu.VMEM)
    return pl.pallas_call(
        output_kernel,
        out_shape=jax.ShapeDtypeStruct((OWNERS, block_rows // 2, columns), f32),
        in_specs=[vmem, pl.BlockSpec(memory_space=pl.ANY)],
        out_specs=vmem,
        scratch_shapes=[
            pltpu.VMEM((columns, w_out.shape[0]), w_out.dtype),
            pltpu.VMEM((pieces, OWNERS, block_rows, width), block.dtype),
            pltpu.VMEM((OWNERS * block_rows, columns), f32),
            pltpu.VMEM((OWNERS * block_rows, columns), f32),
            pltpu.VMEM((OWNERS, block_rows // 2, columns), f32),
            pltpu.SemaphoreType.DMA,
            pltpu.SemaphoreType.DMA((pieces,)),
            pltpu.SemaphoreType.DMA((pieces, OWNERS)),
            pltpu.SemaphoreType.DMA((pieces, OWNERS)),
            pltpu.SemaphoreType.DMA((OWNERS,)),
            pltpu.SemaphoreType.DMA((OWNERS,)),
        ],
        compiler_params=pltpu.CompilerParams(
            collective_id=1, has_side_effects=True, vmem_limit_bytes=VMEM_BYTES
        ),
    )(block, w_out.T)


def body(
    direct,
    hidden,
    norm_gain,
    query_gain,
    key_gain,
    w_query,
    w_key,
    w_value,
    w_out,
    cache_k,
    cache_v,
    lengths,
):
    step_total, row_count, model_width = hidden.shape
    own_rows = step_total * row_count
    head_size = query_gain.shape[0]
    query_width, key_width = w_query.shape[1], w_key.shape[1]
    residual = hidden.astype(jnp.float32)
    normed = rms_scale(residual, norm_gain).astype(jnp.bfloat16).reshape(own_rows, model_width)
    if direct:
        blocks = normed.astype(jnp.float32).reshape(own_rows, OWNERS, -1).transpose(1, 0, 2)
        projected = project(blocks, w_query, w_key, w_value)
    else:
        slab = lax.all_to_all(normed, ring, split_axis=1, concat_axis=0, tiled=True)
        partial_sums = jnp.concatenate(
            [
                jnp.dot(slab, weight, preferred_element_type=jnp.float32)
                for weight in (w_query, w_key, w_value)
            ],
            axis=1,
        )
        projected = lax.psum_scatter(partial_sums, ring, scatter_dimension=0, tiled=True)
    projected = projected.astype(jnp.bfloat16)
    q_heads = projected[:, :query_width].astype(jnp.float32)
    k_heads = projected[:, query_width : query_width + key_width].astype(jnp.float32)
    fresh_v = projected[:, query_width + key_width :]
    positions = lengths.astype(jnp.float32)[None, :] + jnp.arange(step_total, dtype=jnp.float32)[:, None]
    q_heads = q_heads.reshape(step_total, row_count, -1, head_size)
    k_heads = k_heads.reshape(step_total, row_count, -1, head_size)
    queries = rotate(rms_scale(q_heads, query_gain), positions).astype(jnp.bfloat16)
    fresh_k = rotate(rms_scale(k_heads, key_gain), positions).astype(jnp.bfloat16)
    fresh_v = fresh_v.reshape(step_total, row_count, -1, head_size)
    attended = attend(queries, cache_k, cache_v, lengths, fresh_k, fresh_v)
    if direct:
        halves = attended.reshape(own_rows, 2, PIECES, -1).transpose(2, 1, 0, 3)
        halves = halves.reshape(PIECES, 2 * own_rows, -1)
        update = output(halves, w_out).transpose(1, 0, 2)
    else:
        everyone = lax.all_gather(attended, ring, axis=0, tiled=True)
        columns = jnp.dot(everyone, w_out, preferred_element_type=jnp.float32)
        update = lax.all_to_all(columns, ring, split_axis=0, concat_axis=1, tiled=True)
    update = update.reshape(step_total, row_count, model_width)
    return (residual + update).astype(jnp.bfloat16)


def solution(mesh):
    placed = (
        P(None, ("groups", "tensor", "side"), None),
        P(),
        P(),
        P(),
        P(("tensor", "side"), None),
        P(("tensor", "side"), None),
        P(("tensor", "side"), None),
        P(None, ("tensor", "side")),
        P(("groups", "tensor", "side"), None, None, None),
        P(("groups", "tensor", "side"), None, None, None),
        P(("groups", "tensor", "side")),
    )
    direct = mesh.shape["tensor"] == LONG * SHORT and mesh.shape["side"] == SIDE
    return jax.shard_map(
        functools.partial(body, direct),
        mesh=mesh,
        in_specs=placed,
        out_specs=P(None, ("groups", "tensor", "side"), None),
        check_vma=False,
    )
```

```python
import functools

import jax
import jax.numpy as jnp
from jax import lax
from jax.experimental import pallas as pl
from jax.experimental.pallas import tpu as pltpu
from jax.sharding import PartitionSpec as P

rope_base = 1000000.0
norm_eps = 1e-06
masked_score = -1e30
ring = ("tensor", "side")


def rms_scale(values, gain_vector):
    mean_square = jnp.mean(values * values, axis=-1, keepdims=True)
    return values * lax.rsqrt(mean_square + norm_eps) * gain_vector


def rotate(values, positions):
    half_dim = values.shape[-1] // 2
    frequency = rope_base ** (-2.0 * jnp.arange(half_dim, dtype=jnp.float32) / values.shape[-1])
    angles = positions[..., None] * frequency
    cosine = jnp.cos(angles)[..., None, :]
    sine_part = jnp.sin(angles)[..., None, :]
    lower_half = values[..., :half_dim]
    upper_half = values[..., half_dim:]
    return jnp.concatenate(
        [
            lower_half * cosine - upper_half * sine_part,
            upper_half * cosine + lower_half * sine_part,
        ],
        axis=-1,
    )


def attend(queries, cache_k, cache_v, lengths, fresh_k, fresh_v):
    step_total, row_count, head_count, head_size = queries.shape
    kv_count, context = cache_k.shape[1:3]
    group = head_count // kv_count
    grouped = queries.reshape(step_total, row_count, kv_count, group, head_size)
    grouped = grouped.transpose(1, 2, 0, 3, 4).reshape(
        row_count, kv_count, step_total * group, head_size
    )
    fresh_k = fresh_k.transpose(1, 2, 0, 3)
    fresh_v = fresh_v.transpose(1, 2, 0, 3)
    score_scale = head_size ** (-0.5)
    cached_scores = (
        jnp.einsum("rkqd,rkld->rkql", grouped, cache_k, preferred_element_type=jnp.float32)
        * score_scale
    )
    live_mask = jnp.arange(context, dtype=jnp.int32)[None, :] < lengths[:, None]
    cached_scores = jnp.where(live_mask[:, None, None, :], cached_scores, masked_score)
    fresh_scores = (
        jnp.einsum("rkqd,rksd->rkqs", grouped, fresh_k, preferred_element_type=jnp.float32)
        * score_scale
    )
    query_step = jnp.arange(step_total * group, dtype=jnp.int32) // group
    causal = jnp.arange(step_total, dtype=jnp.int32)[None, :] <= query_step[:, None]
    fresh_scores = jnp.where(causal, fresh_scores, masked_score)
    highest = jnp.maximum(jnp.max(cached_scores, axis=-1), jnp.max(fresh_scores, axis=-1))[
        ..., None
    ]
    cached_exp = jnp.exp(cached_scores - highest)
    fresh_exp = jnp.exp(fresh_scores - highest)
    denominator = jnp.sum(cached_exp, axis=-1, keepdims=True) + jnp.sum(
        fresh_exp, axis=-1, keepdims=True
    )
    cached_weight = (cached_exp / denominator).astype(jnp.bfloat16)
    fresh_weight = (fresh_exp / denominator).astype(jnp.bfloat16)
    mixed_out = jnp.einsum(
        "rkql,rkld->rkqd", cached_weight, cache_v, preferred_element_type=jnp.float32
    )
    mixed_out = mixed_out + jnp.einsum(
        "rkqs,rksd->rkqd", fresh_weight, fresh_v, preferred_element_type=jnp.float32
    )
    mixed_out = mixed_out.astype(jnp.bfloat16)
    mixed_out = mixed_out.reshape(row_count, kv_count, step_total, group, head_size)
    return mixed_out.transpose(2, 0, 1, 3, 4).reshape(
        step_total * row_count, head_count * head_size
    )


LONG, SHORT, SIDE = 4, 2, 2
OWNERS = LONG * SHORT * SIDE
PIECES = 4
VMEM_BYTES = 56 * 1024 * 1024


def place():
    tensor_index = lax.axis_index("tensor")
    return tensor_index // SHORT, lax.rem(tensor_index, SHORT), lax.axis_index("side")


def others():
    return [
        (a, b, c)
        for a in range(LONG)
        for b in range(SHORT)
        for c in range(SIDE)
        if (a, b, c) != (0, 0, 0)
    ]


def slot(step):
    a, b, c = step
    return (a * SHORT + b) * SIDE + c


def shifted(me, step):
    return tuple(
        lax.rem(i + d, n) for i, d, n in zip(me, step, (LONG, SHORT, SIDE), strict=True)
    )


def device(where):
    return {"tensor": where[0] * SHORT + where[1], "side": where[2]}


def number(where):
    return (where[0] * SHORT + where[1]) * SIDE + where[2]


def by_side(where):
    return (where[2] * SHORT + where[1]) * LONG + where[0]


def remote(src, dst, send_sem, recv_sem, where):
    return pltpu.make_async_remote_copy(
        src_ref=src,
        dst_ref=dst,
        send_sem=send_sem,
        recv_sem=recv_sem,
        device_id=device(where),
        device_id_type=pl.DeviceIdType.MESH,
    )


def greet(me):
    barrier = pltpu.get_barrier_semaphore()
    for step in others():
        pl.semaphore_signal(
            barrier,
            inc=1,
            device_id=device(shifted(me, step)),
            device_id_type=pl.DeviceIdType.MESH,
        )
    pl.semaphore_wait(barrier, OWNERS - 1)


def project_kernel(
    width,
    x_ref,
    wq_ref,
    wk_ref,
    wv_ref,
    out_ref,
    wq,
    wk,
    wv,
    slab,
    first,
    from_side,
    second,
    from_short,
    third,
    from_long,
    load_sem,
    slab_send,
    slab_recv,
    send_sem,
    recv_sem,
):
    me = place()
    long_index, short_index, side_index = me
    loads = [
        pltpu.make_async_copy(src, dst, load_sem.at[i])
        for i, (src, dst) in enumerate(((wq_ref, wq), (wk_ref, wk), (wv_ref, wv)))
    ]
    for load in loads:
        load.start()
    greet(me)
    scattered = []
    for step in others():
        target = shifted(me, step)
        copy = remote(
            x_ref.at[number(target)],
            slab.at[by_side(me)],
            slab_send.at[slot(step)],
            slab_recv.at[slot(step)],
            target,
        )
        copy.start()
        scattered.append(copy)
    slab[by_side(me)] = x_ref[number(me)]
    for load in loads:
        load.wait()
    for copy in scattered:
        copy.wait_recv()
    own_rows, depth = slab.shape[1:]
    left = slab[...].reshape(OWNERS * own_rows, depth).astype(jnp.bfloat16)

    pieces = []
    for weight in (wq, wk, wv):
        pieces += [(weight, start) for start in range(0, weight.shape[1], width)]
    total = len(pieces)
    sent = []

    def multiply(c):
        weight, start = pieces[c]
        product = jnp.dot(
            left, weight[:, start : start + width], preferred_element_type=jnp.float32
        )
        first[c] = product.reshape(SIDE, SHORT, LONG, own_rows, width)
        copy = remote(
            first.at[c, 1 - side_index],
            from_side.at[c],
            send_sem.at[c, 0],
            recv_sem.at[c, 0],
            shifted(me, (0, 0, 1)),
        )
        copy.start()
        sent.append(copy)
        return copy

    def add_side(c, arrived):
        arrived.wait_recv()
        second[c] = first[c, side_index] + from_side[c]
        copy = remote(
            second.at[c, 1 - short_index],
            from_short.at[c],
            send_sem.at[c, 1],
            recv_sem.at[c, 1],
            shifted(me, (0, 1, 0)),
        )
        copy.start()
        sent.append(copy)
        return copy

    def add_short(c, arrived):
        arrived.wait_recv()
        third[c] = second[c, short_index] + from_short[c]
        copies = []
        for hop in range(1, LONG):
            target = shifted(me, (hop, 0, 0))
            copy = remote(
                third.at[c, target[0]],
                from_long.at[c, hop - 1],
                send_sem.at[c, 1 + hop],
                recv_sem.at[c, 1 + hop],
                target,
            )
            copy.start()
            copies.append(copy)
        sent.extend(copies)
        return copies

    def add_long(c, arrived):
        value = third[c, long_index]
        for hop, copy in enumerate(arrived):
            copy.wait_recv()
            value = value + from_long[c, hop]
        out_ref[:, c * width : (c + 1) * width] = value

    side_copies = [None] * total
    short_copies = [None] * total
    long_copies = [None] * total
    for tick in range(total + 8):
        if tick < total:
            side_copies[tick] = multiply(tick)
        if 0 <= tick - 1 < total:
            short_copies[tick - 1] = add_side(tick - 1, side_copies[tick - 1])
        if 0 <= tick - 4 < total:
            long_copies[tick - 4] = add_short(tick - 4, short_copies[tick - 4])
        if 0 <= tick - 8 < total:
            add_long(tick - 8, long_copies[tick - 8])
    for copy in scattered + sent:
        copy.wait_send()


def project(blocks, w_query, w_key, w_value):
    own_rows, depth = blocks.shape[1:]
    width = w_key.shape[1] // 2
    columns = w_query.shape[1] + w_key.shape[1] + w_value.shape[1]
    total = columns // width
    f32 = jnp.float32
    hbm = pl.BlockSpec(memory_space=pl.ANY)
    vmem = pl.BlockSpec(memory_space=pltpu.VMEM)
    return pl.pallas_call(
        functools.partial(project_kernel, width),
        out_shape=jax.ShapeDtypeStruct((own_rows, columns), f32),
        in_specs=[vmem, hbm, hbm, hbm],
        out_specs=vmem,
        scratch_shapes=[
            pltpu.VMEM(w_query.shape, w_query.dtype),
            pltpu.VMEM(w_key.shape, w_key.dtype),
            pltpu.VMEM(w_value.shape, w_value.dtype),
            pltpu.VMEM(blocks.shape, f32),
            pltpu.VMEM((total, SIDE, SHORT, LONG, own_rows, width), f32),
            pltpu.VMEM((total, SHORT, LONG, own_rows, width), f32),
            pltpu.VMEM((total, SHORT, LONG, own_rows, width), f32),
            pltpu.VMEM((total, LONG, own_rows, width), f32),
            pltpu.VMEM((total, LONG, own_rows, width), f32),
            pltpu.VMEM((total, LONG - 1, own_rows, width), f32),
            pltpu.SemaphoreType.DMA((3,)),
            pltpu.SemaphoreType.DMA((OWNERS,)),
            pltpu.SemaphoreType.DMA((OWNERS,)),
            pltpu.SemaphoreType.DMA((total, 1 + LONG)),
            pltpu.SemaphoreType.DMA((total, 1 + LONG)),
        ],
        compiler_params=pltpu.CompilerParams(
            collective_id=0, has_side_effects=True, vmem_limit_bytes=VMEM_BYTES
        ),
    )(blocks, w_query, w_key, w_value)


def output_kernel(
    x_ref,
    w_ref,
    out_ref,
    weight,
    gathered,
    low,
    high,
    result,
    load_sem,
    own_sem,
    send_sem,
    recv_sem,
    back_send,
    back_recv,
):
    me = place()
    pieces, owners, block_rows, width = gathered.shape
    load = pltpu.make_async_copy(w_ref, weight, load_sem)
    load.start()
    own = [
        pltpu.make_async_copy(x_ref.at[p], gathered.at[p, number(me)], own_sem.at[p])
        for p in range(pieces)
    ]
    for copy in own:
        copy.start()
    greet(me)
    for copy in own:
        copy.wait()
    copies = {}

    def pass_on(p, origin_step, step):
        behind = tuple((n - d) % n for d, n in zip(origin_step, (LONG, SHORT, SIDE)))
        block = gathered.at[p, number(shifted(me, behind))]
        arrival = tuple(o + d for o, d in zip(origin_step, step))
        copy = remote(
            block,
            block,
            send_sem.at[p, slot(arrival)],
            recv_sem.at[p, slot(arrival)],
            shifted(me, step),
        )
        copy.start()
        copies[p, arrival] = copy

    def start_own(p):
        for hop in (2, 1, 3):
            pass_on(p, (0, 0, 0), (hop, 0, 0))
        pass_on(p, (0, 0, 0), (0, 1, 0))
        pass_on(p, (0, 0, 0), (0, 0, 1))

    def pass_long(p):
        for hop in (1, 3, 2):
            copies[p, (hop, 0, 0)].wait_recv()
            pass_on(p, (hop, 0, 0), (0, 1, 0))
            pass_on(p, (hop, 0, 0), (0, 0, 1))

    def pass_short(p):
        for hop in (0, 1, 3, 2):
            copies[p, (hop, 1, 0)].wait_recv()
            pass_on(p, (hop, 1, 0), (0, 0, 1))

    def multiply(p):
        for hop in range(LONG):
            for short in range(SHORT):
                copies[p, (hop, short, 1)].wait_recv()
        left = gathered[p].reshape(owners * block_rows, width)
        for total, start in ((low, p * width), (high, (pieces + p) * width)):
            product = lax.dot_general(
                left,
                weight[:, start : start + width],
                (((1,), (1,)), ((), ())),
                preferred_element_type=jnp.float32,
            )
            total[...] = product if p == 0 else total[...] + product

    for p in range(pieces):
        start_own(p)
    for tick in range(pieces + 2):
        if tick < pieces:
            pass_long(tick)
        if 0 <= tick - 1 < pieces:
            pass_short(tick - 1)
        if tick == 2:
            load.wait()
        if 0 <= tick - 2 < pieces:
            multiply(tick - 2)

    own_rows = block_rows // 2
    wide = (owners, block_rows, low.shape[1])
    result[...] = (
        low[...].reshape(wide)[:, :own_rows] + high[...].reshape(wide)[:, own_rows:]
    )
    returned = []
    for step in others():
        target = shifted(me, step)
        copy = remote(
            result.at[number(target)],
            out_ref.at[number(me)],
            back_send.at[slot(step)],
            back_recv.at[slot(step)],
            target,
        )
        copy.start()
        returned.append(copy)
    out_ref[number(me)] = result[number(me)]
    for copy in returned:
        copy.wait_recv()
    for copy in list(copies.values()) + returned:
        copy.wait_send()


def output(block, w_out):
    pieces, block_rows, width = block.shape
    columns = w_out.shape[1]
    f32 = jnp.float32
    vmem = pl.BlockSpec(memory_space=pltpu.VMEM)
    return pl.pallas_call(
        output_kernel,
        out_shape=jax.ShapeDtypeStruct((OWNERS, block_rows // 2, columns), f32),
        in_specs=[vmem, pl.BlockSpec(memory_space=pl.ANY)],
        out_specs=vmem,
        scratch_shapes=[
            pltpu.VMEM((columns, w_out.shape[0]), w_out.dtype),
            pltpu.VMEM((pieces, OWNERS, block_rows, width), block.dtype),
            pltpu.VMEM((OWNERS * block_rows, columns), f32),
            pltpu.VMEM((OWNERS * block_rows, columns), f32),
            pltpu.VMEM((OWNERS, block_rows // 2, columns), f32),
            pltpu.SemaphoreType.DMA,
            pltpu.SemaphoreType.DMA((pieces,)),
            pltpu.SemaphoreType.DMA((pieces, OWNERS)),
            pltpu.SemaphoreType.DMA((pieces, OWNERS)),
            pltpu.SemaphoreType.DMA((OWNERS,)),
            pltpu.SemaphoreType.DMA((OWNERS,)),
        ],
        compiler_params=pltpu.CompilerParams(
            collective_id=1, has_side_effects=True, vmem_limit_bytes=VMEM_BYTES
        ),
    )(block, w_out.T)


def body(
    direct,
    hidden,
    norm_gain,
    query_gain,
    key_gain,
    w_query,
    w_key,
    w_value,
    w_out,
    cache_k,
    cache_v,
    lengths,
):
    step_total, row_count, model_width = hidden.shape
    own_rows = step_total * row_count
    head_size = query_gain.shape[0]
    query_width, key_width = w_query.shape[1], w_key.shape[1]
    residual = hidden.astype(jnp.float32)
    normed = rms_scale(residual, norm_gain).astype(jnp.bfloat16).reshape(own_rows, model_width)
    if direct:
        blocks = normed.astype(jnp.float32).reshape(own_rows, OWNERS, -1).transpose(1, 0, 2)
        projected = project(blocks, w_query, w_key, w_value)
    else:
        slab = lax.all_to_all(normed, ring, split_axis=1, concat_axis=0, tiled=True)
        partial_sums = jnp.concatenate(
            [
                jnp.dot(slab, weight, preferred_element_type=jnp.float32)
                for weight in (w_query, w_key, w_value)
            ],
            axis=1,
        )
        projected = lax.psum_scatter(partial_sums, ring, scatter_dimension=0, tiled=True)
    projected = projected.astype(jnp.bfloat16)
    q_heads = projected[:, :query_width].astype(jnp.float32)
    k_heads = projected[:, query_width : query_width + key_width].astype(jnp.float32)
    fresh_v = projected[:, query_width + key_width :]
    positions = lengths.astype(jnp.float32)[None, :] + jnp.arange(step_total, dtype=jnp.float32)[:, None]
    q_heads = q_heads.reshape(step_total, row_count, -1, head_size)
    k_heads = k_heads.reshape(step_total, row_count, -1, head_size)
    queries = rotate(rms_scale(q_heads, query_gain), positions).astype(jnp.bfloat16)
    fresh_k = rotate(rms_scale(k_heads, key_gain), positions).astype(jnp.bfloat16)
    fresh_v = fresh_v.reshape(step_total, row_count, -1, head_size)
    attended = attend(queries, cache_k, cache_v, lengths, fresh_k, fresh_v)
    if direct:
        halves = attended.reshape(own_rows, 2, PIECES, -1).transpose(2, 1, 0, 3)
        halves = halves.reshape(PIECES, 2 * own_rows, -1)
        update = output(halves, w_out).transpose(1, 0, 2)
    else:
        everyone = lax.all_gather(attended, ring, axis=0, tiled=True)
        columns = jnp.dot(everyone, w_out, preferred_element_type=jnp.float32)
        update = lax.all_to_all(columns, ring, split_axis=0, concat_axis=1, tiled=True)
    update = update.reshape(step_total, row_count, model_width)
    return (residual + update).astype(jnp.bfloat16)


def solution(mesh):
    placed = (
        P(None, ("groups", "tensor", "side"), None),
        P(),
        P(),
        P(),
        P(("tensor", "side"), None),
        P(("tensor", "side"), None),
        P(("tensor", "side"), None),
        P(None, ("tensor", "side")),
        P(("groups", "tensor", "side"), None, None, None),
        P(("groups", "tensor", "side"), None, None, None),
        P(("groups", "tensor", "side")),
    )
    direct = mesh.shape["tensor"] == LONG * SHORT and mesh.shape["side"] == SIDE
    return jax.shard_map(
        functools.partial(body, direct),
        mesh=mesh,
        in_specs=placed,
        out_specs=P(None, ("groups", "tensor", "side"), None),
        check_vma=False,
    )
```

```python
import functools

import jax
import jax.numpy as jnp
from jax import lax
from jax.experimental import pallas as pl
from jax.experimental.pallas import tpu as pltpu
from jax.sharding import PartitionSpec as P

rope_base = 1000000.0
norm_eps = 1e-06
masked_score = -1e30
ring = ("tensor", "side")


def rms_scale(values, gain_vector):
    mean_square = jnp.mean(values * values, axis=-1, keepdims=True)
    return values * lax.rsqrt(mean_square + norm_eps) * gain_vector


def rotate(values, positions):
    half_dim = values.shape[-1] // 2
    frequency = rope_base ** (-2.0 * jnp.arange(half_dim, dtype=jnp.float32) / values.shape[-1])
    angles = positions[..., None] * frequency
    cosine = jnp.cos(angles)[..., None, :]
    sine_part = jnp.sin(angles)[..., None, :]
    lower_half = values[..., :half_dim]
    upper_half = values[..., half_dim:]
    return jnp.concatenate(
        [
            lower_half * cosine - upper_half * sine_part,
            upper_half * cosine + lower_half * sine_part,
        ],
        axis=-1,
    )


def attend(queries, cache_k, cache_v, lengths, fresh_k, fresh_v):
    step_total, row_count, head_count, head_size = queries.shape
    kv_count, context = cache_k.shape[1:3]
    group = head_count // kv_count
    grouped = queries.reshape(step_total, row_count, kv_count, group, head_size)
    grouped = grouped.transpose(1, 2, 0, 3, 4).reshape(
        row_count, kv_count, step_total * group, head_size
    )
    fresh_k = fresh_k.transpose(1, 2, 0, 3)
    fresh_v = fresh_v.transpose(1, 2, 0, 3)
    score_scale = head_size ** (-0.5)
    cached_scores = (
        jnp.einsum("rkqd,rkld->rkql", grouped, cache_k, preferred_element_type=jnp.float32)
        * score_scale
    )
    live_mask = jnp.arange(context, dtype=jnp.int32)[None, :] < lengths[:, None]
    cached_scores = jnp.where(live_mask[:, None, None, :], cached_scores, masked_score)
    fresh_scores = (
        jnp.einsum("rkqd,rksd->rkqs", grouped, fresh_k, preferred_element_type=jnp.float32)
        * score_scale
    )
    query_step = jnp.arange(step_total * group, dtype=jnp.int32) // group
    causal = jnp.arange(step_total, dtype=jnp.int32)[None, :] <= query_step[:, None]
    fresh_scores = jnp.where(causal, fresh_scores, masked_score)
    highest = jnp.maximum(jnp.max(cached_scores, axis=-1), jnp.max(fresh_scores, axis=-1))[
        ..., None
    ]
    cached_exp = jnp.exp(cached_scores - highest)
    fresh_exp = jnp.exp(fresh_scores - highest)
    denominator = jnp.sum(cached_exp, axis=-1, keepdims=True) + jnp.sum(
        fresh_exp, axis=-1, keepdims=True
    )
    cached_weight = (cached_exp / denominator).astype(jnp.bfloat16)
    fresh_weight = (fresh_exp / denominator).astype(jnp.bfloat16)
    mixed_out = jnp.einsum(
        "rkql,rkld->rkqd", cached_weight, cache_v, preferred_element_type=jnp.float32
    )
    mixed_out = mixed_out + jnp.einsum(
        "rkqs,rksd->rkqd", fresh_weight, fresh_v, preferred_element_type=jnp.float32
    )
    mixed_out = mixed_out.astype(jnp.bfloat16)
    mixed_out = mixed_out.reshape(row_count, kv_count, step_total, group, head_size)
    return mixed_out.transpose(2, 0, 1, 3, 4).reshape(
        step_total * row_count, head_count * head_size
    )


LONG, SHORT, SIDE = 4, 2, 2
OWNERS = LONG * SHORT * SIDE
PIECES = 4
VMEM_BYTES = 56 * 1024 * 1024


def place():
    tensor_index = lax.axis_index("tensor")
    return tensor_index // SHORT, lax.rem(tensor_index, SHORT), lax.axis_index("side")


def others():
    return [
        (a, b, c)
        for a in range(LONG)
        for b in range(SHORT)
        for c in range(SIDE)
        if (a, b, c) != (0, 0, 0)
    ]


def slot(step):
    a, b, c = step
    return (a * SHORT + b) * SIDE + c


def shifted(me, step):
    return tuple(
        lax.rem(i + d, n) for i, d, n in zip(me, step, (LONG, SHORT, SIDE), strict=True)
    )


def device(where):
    return {"tensor": where[0] * SHORT + where[1], "side": where[2]}


def number(where):
    return (where[0] * SHORT + where[1]) * SIDE + where[2]


def by_side(where):
    pair = lax.rem(where[0], 2) * (LONG // 2) + where[0] // 2
    return (where[2] * SHORT + where[1]) * LONG + pair


def remote(src, dst, send_sem, recv_sem, where):
    return pltpu.make_async_remote_copy(
        src_ref=src,
        dst_ref=dst,
        send_sem=send_sem,
        recv_sem=recv_sem,
        device_id=device(where),
        device_id_type=pl.DeviceIdType.MESH,
    )


def greet(me):
    barrier = pltpu.get_barrier_semaphore()
    for step in others():
        pl.semaphore_signal(
            barrier,
            inc=1,
            device_id=device(shifted(me, step)),
            device_id_type=pl.DeviceIdType.MESH,
        )
    pl.semaphore_wait(barrier, OWNERS - 1)


def project_kernel(
    width,
    x_ref,
    wq_ref,
    wk_ref,
    wv_ref,
    out_ref,
    wq,
    wk,
    wv,
    slab,
    first,
    from_side,
    second,
    from_short,
    third,
    from_near,
    fourth,
    from_long,
    load_sem,
    slab_send,
    slab_recv,
    send_sem,
    recv_sem,
):
    me = place()
    long_index, short_index, side_index = me
    upper, odd = long_index // 2, lax.rem(long_index, 2)
    loads = [
        pltpu.make_async_copy(src, dst, load_sem.at[i])
        for i, (src, dst) in enumerate(((wq_ref, wq), (wk_ref, wk), (wv_ref, wv)))
    ]
    for load in loads:
        load.start()
    greet(me)
    scattered = []
    for step in others():
        target = shifted(me, step)
        copy = remote(
            x_ref.at[number(target)],
            slab.at[by_side(me)],
            slab_send.at[slot(step)],
            slab_recv.at[slot(step)],
            target,
        )
        copy.start()
        scattered.append(copy)
    slab[by_side(me)] = x_ref[number(me)]
    for load in loads:
        load.wait()
    for copy in scattered:
        copy.wait_recv()
    own_rows, depth = slab.shape[1:]
    left = slab[...].reshape(OWNERS * own_rows, depth).astype(jnp.bfloat16)

    pieces = []
    for weight in (wq, wk, wv):
        pieces += [(weight, start) for start in range(0, weight.shape[1], width)]
    total = len(pieces)
    sent = []

    def multiply(c):
        weight, start = pieces[c]
        product = jnp.dot(
            left, weight[:, start : start + width], preferred_element_type=jnp.float32
        )
        first[c] = product.reshape(SIDE, SHORT, 2, LONG // 2, own_rows, width)
        copy = remote(
            first.at[c, 1 - side_index],
            from_side.at[c],
            send_sem.at[c, 0],
            recv_sem.at[c, 0],
            shifted(me, (0, 0, 1)),
        )
        copy.start()
        sent.append(copy)
        return copy

    def add_side(c, arrived):
        arrived.wait_recv()
        second[c] = first[c, side_index] + from_side[c]
        copy = remote(
            second.at[c, 1 - short_index],
            from_short.at[c],
            send_sem.at[c, 1],
            recv_sem.at[c, 1],
            shifted(me, (0, 1, 0)),
        )
        copy.start()
        sent.append(copy)
        return copy

    def add_short(c, arrived):
        arrived.wait_recv()
        third[c] = second[c, short_index] + from_short[c]
        copy = remote(
            third.at[c, 1 - odd],
            from_near.at[c],
            send_sem.at[c, 2],
            recv_sem.at[c, 2],
            (long_index + 1 - 2 * odd, short_index, side_index),
        )
        copy.start()
        sent.append(copy)
        return copy

    def add_near(c, arrived):
        arrived.wait_recv()
        fourth[c] = third[c, odd] + from_near[c]
        copy = remote(
            fourth.at[c, 1 - upper],
            from_long.at[c],
            send_sem.at[c, 3],
            recv_sem.at[c, 3],
            shifted(me, (2, 0, 0)),
        )
        copy.start()
        sent.append(copy)
        return copy

    def add_long(c, arrived):
        arrived.wait_recv()
        out_ref[:, c * width : (c + 1) * width] = fourth[c, upper] + from_long[c]

    side_copies = [None] * total
    short_copies = [None] * total
    near_copies = [None] * total
    long_copies = [None] * total
    for tick in range(total + 8):
        if tick < total:
            side_copies[tick] = multiply(tick)
        if 0 <= tick - 1 < total:
            short_copies[tick - 1] = add_side(tick - 1, side_copies[tick - 1])
        if 0 <= tick - 4 < total:
            near_copies[tick - 4] = add_short(tick - 4, short_copies[tick - 4])
        if 0 <= tick - 6 < total:
            long_copies[tick - 6] = add_near(tick - 6, near_copies[tick - 6])
        if 0 <= tick - 8 < total:
            add_long(tick - 8, long_copies[tick - 8])
    for copy in scattered + sent:
        copy.wait_send()


def project(blocks, w_query, w_key, w_value):
    own_rows, depth = blocks.shape[1:]
    width = w_key.shape[1] // 2
    columns = w_query.shape[1] + w_key.shape[1] + w_value.shape[1]
    total = columns // width
    f32 = jnp.float32
    hbm = pl.BlockSpec(memory_space=pl.ANY)
    vmem = pl.BlockSpec(memory_space=pltpu.VMEM)
    return pl.pallas_call(
        functools.partial(project_kernel, width),
        out_shape=jax.ShapeDtypeStruct((own_rows, columns), f32),
        in_specs=[vmem, hbm, hbm, hbm],
        out_specs=vmem,
        scratch_shapes=[
            pltpu.VMEM(w_query.shape, w_query.dtype),
            pltpu.VMEM(w_key.shape, w_key.dtype),
            pltpu.VMEM(w_value.shape, w_value.dtype),
            pltpu.VMEM(blocks.shape, f32),
            pltpu.VMEM((total, SIDE, SHORT, 2, LONG // 2, own_rows, width), f32),
            pltpu.VMEM((total, SHORT, 2, LONG // 2, own_rows, width), f32),
            pltpu.VMEM((total, SHORT, 2, LONG // 2, own_rows, width), f32),
            pltpu.VMEM((total, 2, LONG // 2, own_rows, width), f32),
            pltpu.VMEM((total, 2, LONG // 2, own_rows, width), f32),
            pltpu.VMEM((total, LONG // 2, own_rows, width), f32),
            pltpu.VMEM((total, LONG // 2, own_rows, width), f32),
            pltpu.VMEM((total, own_rows, width), f32),
            pltpu.SemaphoreType.DMA((3,)),
            pltpu.SemaphoreType.DMA((OWNERS,)),
            pltpu.SemaphoreType.DMA((OWNERS,)),
            pltpu.SemaphoreType.DMA((total, 1 + LONG)),
            pltpu.SemaphoreType.DMA((total, 1 + LONG)),
        ],
        compiler_params=pltpu.CompilerParams(
            collective_id=0, has_side_effects=True, vmem_limit_bytes=VMEM_BYTES
        ),
    )(blocks, w_query, w_key, w_value)


def output_kernel(
    x_ref,
    w_ref,
    out_ref,
    weight,
    gathered,
    low,
    high,
    result,
    load_sem,
    own_sem,
    send_sem,
    recv_sem,
    back_send,
    back_recv,
):
    me = place()
    pieces, owners, block_rows, width = gathered.shape
    load = pltpu.make_async_copy(w_ref, weight, load_sem)
    load.start()
    own = [
        pltpu.make_async_copy(x_ref.at[p], gathered.at[p, number(me)], own_sem.at[p])
        for p in range(pieces)
    ]
    for copy in own:
        copy.start()
    greet(me)
    for copy in own:
        copy.wait()
    copies = {}

    def pass_on(p, origin_step, step):
        behind = tuple((n - d) % n for d, n in zip(origin_step, (LONG, SHORT, SIDE)))
        block = gathered.at[p, number(shifted(me, behind))]
        arrival = tuple(o + d for o, d in zip(origin_step, step))
        copy = remote(
            block,
            block,
            send_sem.at[p, slot(arrival)],
            recv_sem.at[p, slot(arrival)],
            shifted(me, step),
        )
        copy.start()
        copies[p, arrival] = copy

    def start_own(p):
        for hop in (2, 1, 3):
            pass_on(p, (0, 0, 0), (hop, 0, 0))
        pass_on(p, (0, 0, 0), (0, 1, 0))
        pass_on(p, (0, 0, 0), (0, 0, 1))

    def pass_long(p):
        for hop in (1, 3, 2):
            copies[p, (hop, 0, 0)].wait_recv()
            pass_on(p, (hop, 0, 0), (0, 1, 0))
            pass_on(p, (hop, 0, 0), (0, 0, 1))

    def pass_short(p):
        for hop in (0, 1, 3, 2):
            copies[p, (hop, 1, 0)].wait_recv()
            pass_on(p, (hop, 1, 0), (0, 0, 1))

    def multiply(p):
        for hop in range(LONG):
            for short in range(SHORT):
                copies[p, (hop, short, 1)].wait_recv()
        left = gathered[p].reshape(owners * block_rows, width)
        for total, start in ((low, p * width), (high, (pieces + p) * width)):
            product = lax.dot_general(
                left,
                weight[:, start : start + width],
                (((1,), (1,)), ((), ())),
                preferred_element_type=jnp.float32,
            )
            total[...] = product if p == 0 else total[...] + product

    for p in range(pieces):
        start_own(p)
    for tick in range(pieces + 2):
        if tick < pieces:
            pass_long(tick)
        if 0 <= tick - 1 < pieces:
            pass_short(tick - 1)
        if tick == 2:
            load.wait()
        if 0 <= tick - 2 < pieces:
            multiply(tick - 2)

    own_rows = block_rows // 2
    wide = (owners, block_rows, low.shape[1])
    result[...] = (
        low[...].reshape(wide)[:, :own_rows] + high[...].reshape(wide)[:, own_rows:]
    )
    returned = []
    for step in others():
        target = shifted(me, step)
        copy = remote(
            result.at[number(target)],
            out_ref.at[number(me)],
            back_send.at[slot(step)],
            back_recv.at[slot(step)],
            target,
        )
        copy.start()
        returned.append(copy)
    out_ref[number(me)] = result[number(me)]
    for copy in returned:
        copy.wait_recv()
    for copy in list(copies.values()) + returned:
        copy.wait_send()


def output(block, w_out):
    pieces, block_rows, width = block.shape
    columns = w_out.shape[1]
    f32 = jnp.float32
    vmem = pl.BlockSpec(memory_space=pltpu.VMEM)
    return pl.pallas_call(
        output_kernel,
        out_shape=jax.ShapeDtypeStruct((OWNERS, block_rows // 2, columns), f32),
        in_specs=[vmem, pl.BlockSpec(memory_space=pl.ANY)],
        out_specs=vmem,
        scratch_shapes=[
            pltpu.VMEM((columns, w_out.shape[0]), w_out.dtype),
            pltpu.VMEM((pieces, OWNERS, block_rows, width), block.dtype),
            pltpu.VMEM((OWNERS * block_rows, columns), f32),
            pltpu.VMEM((OWNERS * block_rows, columns), f32),
            pltpu.VMEM((OWNERS, block_rows // 2, columns), f32),
            pltpu.SemaphoreType.DMA,
            pltpu.SemaphoreType.DMA((pieces,)),
            pltpu.SemaphoreType.DMA((pieces, OWNERS)),
            pltpu.SemaphoreType.DMA((pieces, OWNERS)),
            pltpu.SemaphoreType.DMA((OWNERS,)),
            pltpu.SemaphoreType.DMA((OWNERS,)),
        ],
        compiler_params=pltpu.CompilerParams(
            collective_id=1, has_side_effects=True, vmem_limit_bytes=VMEM_BYTES
        ),
    )(block, w_out.T)


def body(
    direct,
    hidden,
    norm_gain,
    query_gain,
    key_gain,
    w_query,
    w_key,
    w_value,
    w_out,
    cache_k,
    cache_v,
    lengths,
):
    step_total, row_count, model_width = hidden.shape
    own_rows = step_total * row_count
    head_size = query_gain.shape[0]
    query_width, key_width = w_query.shape[1], w_key.shape[1]
    residual = hidden.astype(jnp.float32)
    normed = rms_scale(residual, norm_gain).astype(jnp.bfloat16).reshape(own_rows, model_width)
    if direct:
        blocks = normed.astype(jnp.float32).reshape(own_rows, OWNERS, -1).transpose(1, 0, 2)
        projected = project(blocks, w_query, w_key, w_value)
    else:
        slab = lax.all_to_all(normed, ring, split_axis=1, concat_axis=0, tiled=True)
        partial_sums = jnp.concatenate(
            [
                jnp.dot(slab, weight, preferred_element_type=jnp.float32)
                for weight in (w_query, w_key, w_value)
            ],
            axis=1,
        )
        projected = lax.psum_scatter(partial_sums, ring, scatter_dimension=0, tiled=True)
    projected = projected.astype(jnp.bfloat16)
    q_heads = projected[:, :query_width].astype(jnp.float32)
    k_heads = projected[:, query_width : query_width + key_width].astype(jnp.float32)
    fresh_v = projected[:, query_width + key_width :]
    positions = lengths.astype(jnp.float32)[None, :] + jnp.arange(step_total, dtype=jnp.float32)[:, None]
    q_heads = q_heads.reshape(step_total, row_count, -1, head_size)
    k_heads = k_heads.reshape(step_total, row_count, -1, head_size)
    queries = rotate(rms_scale(q_heads, query_gain), positions).astype(jnp.bfloat16)
    fresh_k = rotate(rms_scale(k_heads, key_gain), positions).astype(jnp.bfloat16)
    fresh_v = fresh_v.reshape(step_total, row_count, -1, head_size)
    attended = attend(queries, cache_k, cache_v, lengths, fresh_k, fresh_v)
    if direct:
        halves = attended.reshape(own_rows, 2, PIECES, -1).transpose(2, 1, 0, 3)
        halves = halves.reshape(PIECES, 2 * own_rows, -1)
        update = output(halves, w_out).transpose(1, 0, 2)
    else:
        everyone = lax.all_gather(attended, ring, axis=0, tiled=True)
        columns = jnp.dot(everyone, w_out, preferred_element_type=jnp.float32)
        update = lax.all_to_all(columns, ring, split_axis=0, concat_axis=1, tiled=True)
    update = update.reshape(step_total, row_count, model_width)
    return (residual + update).astype(jnp.bfloat16)


def solution(mesh):
    placed = (
        P(None, ("groups", "tensor", "side"), None),
        P(),
        P(),
        P(),
        P(("tensor", "side"), None),
        P(("tensor", "side"), None),
        P(("tensor", "side"), None),
        P(None, ("tensor", "side")),
        P(("groups", "tensor", "side"), None, None, None),
        P(("groups", "tensor", "side"), None, None, None),
        P(("groups", "tensor", "side")),
    )
    direct = mesh.shape["tensor"] == LONG * SHORT and mesh.shape["side"] == SIDE
    return jax.shard_map(
        functools.partial(body, direct),
        mesh=mesh,
        in_specs=placed,
        out_specs=P(None, ("groups", "tensor", "side"), None),
        check_vma=False,
    )
```
